256 devices in a mesh: dp: 4 (over x), expert: 64 (over y, z, core).
Axes of the slice: x: 4, y: 4, z: 8, core: 2. Of those that a mesh axis runs over, the one named last changes fastest.
Arguments:
- tokens: bfloat16 [32768, 2048], P(('dp', 'expert')), may hold values from -6 to 6
- expert_ids: int32 [32768, 4], P(('dp', 'expert')), may hold values from 0 to 63, all different within a row; in each aligned block of 128 rows (0 to 127, 128 to 255, ...) at most 10 rows name the same one
- probs: float32 [32768, 4], P(('dp', 'expert')), may hold values from 0.2 to 1
- trade: int32 [32], replicated, may hold values from 0 to 1, as said below
- gate_weight: bfloat16 [64, 2048, 768], P('expert'), may hold values from -0.125 to 0.125
- up_weight: bfloat16 [64, 2048, 768], P('expert'), may hold values from -0.125 to 0.125
- down_weight: bfloat16 [64, 768, 2048], P('expert'), may hold values from -0.21875 to 0.21875
- out_grad: bfloat16 [32768, 2048], P(('dp', 'expert')), may hold values from -0.29882812 to 0.29882812
Outputs:
- combined: bfloat16 [32768, 2048], P(('dp', 'expert'))
- gate_grad: bfloat16 [64, 2048, 768], P('expert', 'dp')
- up_grad: bfloat16 [64, 2048, 768], P('expert', 'dp')
- down_grad: bfloat16 [64, 768, 2048], P('expert', None, 'dp')
The draws below stay inside these ranges and needn't reach their ends.
Inputs may be any that keep to these rules, and one draw needn't show every extreme that they name: `trade`: index k below 32 pairs expert index k with k + 32; at least one pair trades and at least one does not. `expert_ids`: each row names 4 different experts. Within the 128 rows of one device no expert is named by more than 10 rows, a bound that some block reaches.
All inputs are finite; a program needn't handle non-finite values.
Results may differ from the reference program's by a relative error of at most 0.0095.
Values may be sent and summed in bfloat16 or wider, within the bound.
No kernel may reach another device: no remote copies, remote signals or barrier semaphores. Data moves between devices by JAX's collectives and lax.ppermute only.
A program may use at most 128 MiB of HBM per device.

```python
import math
import jax
import jax.numpy as jnp
import numpy as np
from jax import lax

D = 2048
FF = 768
TOPK = 4
TOK_DEV = 128
EXPERTS = 64
CAP = 10
HALF = 32
ROWS = 640
TOKENS = 32768
N_DP = 4
N_EXPERT = 64


def draw_trade(key, part):
    coins = jax.random.randint(jax.random.fold_in(key, 4391), (HALF,), 0, 2, dtype=jnp.int32)
    order = jax.random.permutation(jax.random.fold_in(key, 5821), HALF)
    coins = coins.at[order[0]].set(1)
    coins = coins.at[order[1]].set(0)
    return coins.astype(jnp.int32)


def steps_of(rng, shape, split, low, top_value):
    level, own = 1.0, jax.random.fold_in(rng, 6)
    for position, blocks in split:
        steps = jnp.exp(jax.random.uniform(jax.random.fold_in(own, position), (blocks,), jnp.float32, low / len(split), top_value / len(split)))
        level = level * jnp.repeat(steps, shape[position] // blocks).reshape([-1 if axis == position else 1 for axis in range(len(shape))])
    return level


def assign_block(key, own, number, rows, amount, top, bound, skew):
    order = jax.random.permutation(key, amount)
    crowded, usual = shares(amount, rows * top, bound, skew, True), shares(amount, rows * top, bound, skew, False)
    places = jnp.arange(amount)

    def named(lengths, offset_by):
        used = int((lengths > 0).sum())
        fixed = max(1, used // 4)
        passed = fixed + (places - fixed + offset_by * (used - fixed)) % max(1, amount - fixed)
        return jnp.zeros((amount,), jnp.int32).at[order[jnp.where(places < fixed, places, passed)]].set(jnp.asarray(lengths, jnp.int32))

    lengths = jnp.where(number % 4 == 0, named(crowded, number // 4), named(usual, number - number // 4 - 1))
    mixed = jax.random.permutation(jax.random.fold_in(own, 3), amount)
    source_of, sink = mixed[0:amount // 2 * 2:2], mixed[1:amount // 2 * 2:2]
    slack = jnp.minimum(lengths[source_of] - 1, bound - lengths[sink]) // 2
    slack = jnp.where((source_of == order[0]) | (sink == order[0]) | (lengths[sink] == 0), 0, jnp.maximum(slack, 0))
    passed = jax.random.randint(jax.random.fold_in(own, 4), (amount // 2,), 0, 1 << 20) % (slack + 1)
    lengths = lengths.at[source_of].add(-passed).at[sink].add(passed)
    members = jnp.searchsorted(jnp.cumsum(lengths), jnp.arange(rows * top), side="right").astype(jnp.int32)
    listing = members.reshape(top, rows).T
    listing = listing[jax.random.permutation(jax.random.fold_in(own, 1), rows)]
    offset_by = jax.random.randint(jax.random.fold_in(own, 2), (rows, 1), 0, top)
    return jnp.take_along_axis(listing, (jnp.arange(top)[None, :] + offset_by) % top, axis=1)


def shares(number_of, total, limit, slope, full):
    portions = [(1 << 20) // math.isqrt(standing ** slope) + 1 for standing in range(1, number_of + 1)]
    largest = limit if full else min(limit, max(-(-total // number_of), total * portions[0] // sum(portions)))
    least = 1 if total - largest >= number_of - 1 else 0
    counts, rest = [largest] + [least] * (number_of - 1), total - largest - least * (number_of - 1)
    while rest > 0:
        movable = [i for i in range(1, number_of) if counts[i] < largest] or [i for i in range(1, number_of) if counts[i] < limit]
        pool, budget = sum([portions[i] for i in movable]), rest
        for i in movable:
            more = min(limit - counts[i], max(1, budget * portions[i] // pool), rest)
            counts[i] = counts[i] + more
            rest = rest - more
    return np.array(counts)


def normal_values(rng, dims, deviation, limit, cuts=(), kind=jnp.bfloat16):
    values = jax.random.normal(rng, dims, jnp.float32) * deviation
    if len(cuts) > 0:
        values = steps_of(rng, dims, cuts, -0.22, 0.18) * values
    return jnp.clip(values, min=-limit, max=limit).astype(kind)


def setup_inputs(seed: int = 0) -> dict:
    key_list = jax.random.split(jax.random.key(seed), 9)
    tokens = normal_values(key_list[0], (TOKENS, D), 1.0, 6.0, ((0, 256),))
    expert_ids_keys = jax.random.split(jax.random.fold_in(key_list[1], 1), TOKENS // TOK_DEV)
    expert_ids_turns = jax.random.permutation(jax.random.fold_in(key_list[1], 3), TOKENS // TOK_DEV)
    expert_ids = jax.vmap(lambda own, number: assign_block(jax.random.fold_in(key_list[1], 2), own, number, TOK_DEV, EXPERTS, TOPK, CAP, 2))(expert_ids_keys, expert_ids_turns).reshape((TOKENS, TOPK))
    probs = jnp.clip(0.2 + 0.8 * jax.random.uniform(key_list[2], (TOKENS, TOPK), jnp.float32) ** steps_of(key_list[2], (TOKENS, TOPK), ((0, 256),), -0.2, 0.2), 0.2, 1.0)
    trade = draw_trade(jax.random.fold_in(key_list[8], 71), 0)
    gate_weight = normal_values(key_list[4], (EXPERTS, D, FF), D ** -0.5, 0.125, ((0, 64),))
    up_weight = normal_values(key_list[5], (EXPERTS, D, FF), D ** -0.5, 0.125, ((0, 64),))
    down_weight = normal_values(key_list[6], (EXPERTS, FF, D), FF ** -0.5, 0.21875, ((0, 64),))
    out_grad = normal_values(key_list[7], (TOKENS, D), 0.05, 0.29882812, ((0, 256),))
    return {"tokens": tokens, "expert_ids": expert_ids, "probs": probs, "trade": trade, "gate_weight": gate_weight, "up_weight": up_weight, "down_weight": down_weight, "out_grad": out_grad}


def rounded(value):
    return lax.optimization_barrier(value.astype(jnp.bfloat16)).astype(jnp.float32)


def slot_numbers(expert_ids):
    sources = N_DP * N_EXPERT
    pair_count = TOK_DEV * TOPK
    chosen = expert_ids.reshape(sources, pair_count).astype(jnp.int32)
    numbers = jnp.arange(EXPERTS, dtype=jnp.int32)
    onehot = (chosen[:, :, None] == numbers[None, None, :]).astype(jnp.int32)
    earlier = jnp.cumsum(onehot, axis=1) - onehot
    placed = jnp.sum(earlier * onehot, axis=2).astype(jnp.int32)
    return (chosen * CAP + placed).astype(jnp.int32)


def reference(tokens, expert_ids, probs, trade, gate_weight, up_weight, down_weight, out_grad):
    sources = N_DP * N_EXPERT
    pair_count = TOK_DEV * TOPK
    slots = slot_numbers(expert_ids)
    pair_ids = jnp.arange(sources * pair_count, dtype=jnp.int32).reshape(sources, pair_count)
    source_ids = jnp.arange(sources, dtype=jnp.int32)[:, None]
    table = jnp.full((sources, EXPERTS * CAP), -1, jnp.int32).at[source_ids, slots].set(pair_ids)
    table = table.reshape(sources, EXPERTS, CAP).transpose(1, 0, 2).reshape(EXPERTS, sources * CAP)
    numbers = jnp.arange(EXPERTS, dtype=jnp.int32)
    halfway = EXPERTS // 2
    owners = jnp.where(trade[numbers % halfway] == 1, jnp.bitwise_xor(numbers, halfway), numbers).astype(jnp.int32)
    prob_flat = probs.reshape(-1)

    def expert_step(combined_sum, inputs):
        pairs, owner = inputs
        live = pairs >= 0
        safe_pairs = jnp.where(live, pairs, 0).astype(jnp.int32)
        token_rows = (safe_pairs // TOPK).astype(jnp.int32)
        weight_col = jnp.where(live, prob_flat[safe_pairs], jnp.zeros((), jnp.float32))
        expert_rows = jnp.where(live[:, None], tokens[token_rows], jnp.zeros((), jnp.bfloat16))
        w_gate = gate_weight[owner]
        w_up = up_weight[owner]
        w_down = down_weight[owner]
        gate_act = jnp.dot(expert_rows, w_gate, preferred_element_type=jnp.float32)
        up_act = jnp.dot(expert_rows, w_up, preferred_element_type=jnp.float32)
        sigma = jax.nn.sigmoid(gate_act)
        silu_gate = gate_act * sigma
        hidden = (silu_gate * up_act).astype(jnp.bfloat16)
        expert_out = jnp.dot(hidden, w_down, preferred_element_type=jnp.float32).astype(jnp.bfloat16)
        combined_sum = combined_sum.at[token_rows].add(weight_col[:, None] * expert_out.astype(jnp.float32))
        out_rows = (weight_col[:, None] * out_grad[token_rows].astype(jnp.float32)).astype(jnp.bfloat16)
        hidden_grad = jnp.dot(out_rows, w_down.T, preferred_element_type=jnp.float32)
        gate_back = (hidden_grad * up_act * (sigma * (1.0 + gate_act * (1.0 - sigma)))).astype(jnp.bfloat16)
        up_back = (hidden_grad * silu_gate).astype(jnp.bfloat16)
        gate_total = jnp.zeros((D, FF), jnp.float32)
        up_total = jnp.zeros((D, FF), jnp.float32)
        down_total = jnp.zeros((FF, D), jnp.float32)
        for replica in range(N_DP):
            lower = replica * ROWS
            part_rows = expert_rows[lower:lower + ROWS]
            gate_total = gate_total + rounded(jnp.dot(part_rows.T, gate_back[lower:lower + ROWS], preferred_element_type=jnp.float32))
            up_total = up_total + rounded(jnp.dot(part_rows.T, up_back[lower:lower + ROWS], preferred_element_type=jnp.float32))
            down_total = down_total + rounded(jnp.dot(hidden[lower:lower + ROWS].T, out_rows[lower:lower + ROWS], preferred_element_type=jnp.float32))
        return combined_sum, (gate_total.astype(jnp.bfloat16), up_total.astype(jnp.bfloat16), down_total.astype(jnp.bfloat16))

    combined_sum, grads = lax.scan(expert_step, jnp.zeros((TOKENS, D), jnp.float32), (table, owners))
    return (combined_sum.astype(jnp.bfloat16), grads[0][owners], grads[1][owners], grads[2][owners])
```

```python
import jax
import jax.numpy as jnp
from jax import lax
from jax.sharding import Mesh
from jax.sharding import PartitionSpec as P

Y, Z, C = "expert_y", "expert_z", "expert_c"
EXPERT = (Y, Z, C)
DP_EXPERT = ("dp",) + EXPERT
F32, BF16, I32 = jnp.float32, jnp.bfloat16, jnp.int32


def dot(a, b, dims=((1,), (0,))):
    return lax.dot_general(a, b, (dims, ((), ())), preferred_element_type=F32)


def local(tokens, expert_ids, probs, trade, gate_weight, up_weight, down_weight, out_grad):
    tok_count, width = tokens.shape
    top_count = expert_ids.shape[1]
    ny, nz, nc = (lax.axis_size(a) for a in EXPERT)
    experts = ny * nz * nc
    halfway = experts // 2
    cap = 5 * tok_count * top_count // (4 * experts)
    peers = ny * nc
    block = nz * cap
    rows = peers * block
    ndp = lax.axis_size("dp")

    all_tokens = lax.all_gather(tokens, Z, axis=0, tiled=True)
    all_grads = lax.all_gather(out_grad, Z, axis=0, tiled=True)

    numbers = jnp.arange(experts, dtype=I32)
    traded = jnp.concatenate([trade, trade]) == 1
    owners = jnp.where(traded, jnp.bitwise_xor(numbers, halfway), numbers)
    ids_t = expert_ids.T
    probs_t = probs.T
    hits = ids_t[:, None, :] == owners[None, :, None]
    named = jnp.any(hits, axis=0)
    weight = jnp.sum(jnp.where(hits, probs_t[:, None, :], 0.0), axis=0)
    before = (
        lax.broadcasted_iota(I32, (tok_count, tok_count), 0)
        < lax.broadcasted_iota(I32, (tok_count, tok_count), 1)
    ).astype(BF16)
    rank = jnp.where(named, dot(named.astype(BF16), before), -1.0)
    by_z = lambda a: a.reshape(ny, nz, nc, tok_count).transpose(1, 0, 2, 3).reshape(nz, peers, tok_count)
    rank_z, weight_z = by_z(rank), by_z(weight)
    info = lax.all_to_all(jnp.concatenate([rank_z, weight_z], axis=1), Z, 0, 0, tiled=True)
    src_rank, src_weight = info[:, :peers], info[:, peers:]
    row_of = jnp.where(
        src_rank >= 0, src_rank + (jnp.arange(nz, dtype=F32) * cap)[:, None, None], -1.0
    ).astype(I32)
    row_of = row_of.transpose(1, 0, 2).reshape(peers, nz * tok_count)
    weight_of = src_weight.transpose(1, 0, 2).reshape(peers, nz * tok_count)
    match = row_of[:, None, :] == jnp.arange(block, dtype=I32)[None, :, None]
    pick = match.astype(BF16).reshape(rows, nz * tok_count)
    row_weight = jnp.sum(jnp.where(match, weight_of[:, None, :], 0.0), axis=2).reshape(rows, 1)

    swap = lambda a: lax.all_to_all(
        a.reshape(peers, block, width), (Y, C), 0, 0, tiled=True
    ).reshape(rows, width)

    expert_rows = swap(dot(pick, all_tokens).astype(BF16))
    out_rows = swap((row_weight * dot(pick, all_grads)).astype(BF16))

    w_gate, w_up, w_down = gate_weight[0], up_weight[0], down_weight[0]
    gate_act = dot(expert_rows, w_gate)
    up_act = dot(expert_rows, w_up)
    sigma = jax.nn.sigmoid(gate_act)
    silu = gate_act * sigma
    hidden = (silu * up_act).astype(BF16)
    expert_out = dot(hidden, w_down).astype(BF16)

    returned = swap(expert_out)
    to = lax.broadcasted_iota(I32, (rows, rows), 0)
    at = lax.broadcasted_iota(I32, (rows, rows), 1)
    moved = (at // block) * cap + (at % block) // cap * (peers * cap) + at % cap
    regroup = (to == moved).astype(BF16)
    returned = dot(regroup, returned).astype(BF16).reshape(nz, peers * cap, width)
    home = lax.all_to_all(returned, Z, 0, 0, tiled=True).reshape(rows, width)
    spread = jnp.where(
        rank_z[:, :, None, :] == jnp.arange(cap, dtype=F32)[None, None, :, None],
        weight_z[:, :, None, :],
        0.0,
    ).reshape(rows, tok_count)
    high = spread.astype(BF16)
    low = (spread - high.astype(F32)).astype(BF16)
    dims = ((0,), (0,))
    combined = (dot(high, home, dims) + dot(low, home, dims)).astype(BF16)

    hidden_grad = dot(out_rows, w_down, ((1,), (1,)))
    gate_back = (hidden_grad * up_act * (sigma * (1.0 + gate_act * (1.0 - sigma)))).astype(BF16)
    up_back = (hidden_grad * silu).astype(BF16)

    share = lambda a: lax.psum_scatter(a, "dp", scatter_dimension=0, tiled=True)
    part = width // ndp
    down_pieces = jnp.stack(
        [dot(hidden, out_rows[:, d * part : (d + 1) * part], dims).astype(BF16) for d in range(ndp)]
    )
    down_part = share(down_pieces)
    gate_part = share(dot(expert_rows, gate_back, dims).astype(BF16))
    up_part = share(dot(expert_rows, up_back, dims).astype(BF16))
    return combined, gate_part[None], up_part[None], down_part


def solution(mesh):
    finer = Mesh(mesh.devices.reshape(mesh.shape["dp"], 4, 8, 2), DP_EXPERT)
    rows = P(DP_EXPERT, None)
    stored = P(EXPERT, None, None)
    return jax.shard_map(
        local,
        mesh=finer,
        in_specs=(rows, rows, rows, P(), stored, stored, stored, rows),
        out_specs=(rows, P(EXPERT, "dp", None), P(EXPERT, "dp", None), P(EXPERT, None, "dp")),
        check_vma=False,
    )
```

```python
import functools

import jax
import jax.numpy as jnp
from jax import lax
from jax.experimental import pallas as pl
from jax.experimental.pallas import tpu as pltpu
from jax.sharding import Mesh
from jax.sharding import PartitionSpec as P

Y, Z, C = "expert_y", "expert_z", "expert_c"
EXPERT = (Y, Z, C)
DP_EXPERT = ("dp",) + EXPERT
F32, BF16, I32 = jnp.float32, jnp.bfloat16, jnp.int32
LANES = 256

PEERS = ((0, 1), (1, 1), (2, 1), (-1, 1), (0, 0), (-1, 0), (1, 0), (2, 0))
GROUPS = ((0, 4), (4, 5), (5, 6), (6, 8))


def dot(a, b, dims=((1,), (0,))):
    return lax.dot_general(a, b, (dims, ((), ())), preferred_element_type=F32)


def turn(a, axis, step):
    n = lax.axis_size(axis)
    return lax.ppermute(a, axis, [(i, (i + step) % n) for i in range(n)])


def ring_order(n):
    return [0] + [s for k in range(1, n // 2) for s in (-k, k)] + [n // 2]


def ring_gather(a, axis):
    n = lax.axis_size(axis)
    cut = a.shape[1] // 2
    up = [a[:, :cut], a[:, cut:]]
    down = list(up)
    blocks = list(up)
    for _ in range(n // 2 - 1):
        for i in range(2):
            up[i] = turn(up[i], axis, 1)
            down[i] = turn(down[i], axis, -1)
        blocks += up + down
    return blocks + [turn(up[0], axis, 1), turn(down[1], axis, -1)]


def swap(other, own, left, right):
    block = own.shape[0]
    right_mine = turn(right, Y, 1)
    left_mine = turn(left, Y, -1)
    got = turn(other, C, 1)
    left_got = turn(got[2 * block :], Y, -1)
    right_got = turn(got[block : 2 * block], Y, 1)
    far_mine = turn(right_mine[block:], Y, 1)
    far_got = turn(left_got[:block], Y, -1)
    return (got, left_got, far_got, right_got, own, right_mine, left_mine, far_mine)


def peer_blocks(refs):
    block = refs[4].shape[0]
    at = (0, 1, 0, 0, 0, 0, 0, 0)
    return [r.at[k * block : (k + 1) * block] for r, k in zip(refs, at)]


def params():
    return pltpu.CompilerParams(vmem_limit_bytes=56 * 2**20)


def cost(flops, moved):
    return pl.CostEstimate(flops=flops, bytes_accessed=moved, transcendentals=0)


def whole():
    return pl.BlockSpec(memory_space=pltpu.VMEM)


def anywhere():
    return pl.BlockSpec(memory_space=pl.ANY)


def match_rows(row_of, j, block):
    numbers = lax.broadcasted_iota(I32, (block, row_of.shape[1]), 0).astype(F32)
    return row_of[j : j + 1, :] == numbers


def pick_kernel(block, weighted, *refs):
    row_ref, weight_ref = refs[:2]
    ins, outs, pick = refs[2:-5], refs[-5:-1], refs[-1]
    weights = []
    for j in range(len(PEERS)):
        match = match_rows(row_ref, j, block)
        pick[j * block : (j + 1) * block, :] = jnp.where(match, 1.0, 0.0).astype(BF16)
        if weighted:
            weights.append(jnp.sum(jnp.where(match, weight_ref[j : j + 1, :], 0.0), axis=1, keepdims=True))
    width = outs[0].shape[1]
    for n in range(0, width, LANES):
        if len(ins) == 1:
            rows = ins[0][:, n : n + LANES]
        else:
            half, at = n // (width // 2), n % (width // 2)
            rows = jnp.concatenate([r[:, at : at + LANES] for r in ins[half::2]], axis=0)
        picked = dot(pick[...], rows)
        if weighted:
            picked = picked * jnp.concatenate(weights, axis=0)
        picked = picked.astype(BF16)
        for out, (lo, hi) in zip(outs, GROUPS):
            out[:, n : n + LANES] = picked[lo * block : hi * block]


def pick_rows(row_of, weight, blocks, block, weighted):
    width = sum(b.shape[1] for b in blocks) * blocks[0].shape[0] // row_of.shape[1]
    rows = len(PEERS) * block
    return pl.pallas_call(
        functools.partial(pick_kernel, block, weighted),
        out_shape=[jax.ShapeDtypeStruct(((hi - lo) * block, width), BF16) for lo, hi in GROUPS],
        in_specs=[whole()] * (2 + len(blocks)),
        out_specs=[whole()] * 4,
        scratch_shapes=[pltpu.VMEM((rows, row_of.shape[1]), BF16)],
        compiler_params=params(),
        cost_estimate=cost(2 * rows * row_of.shape[1] * width, 2 * width * (rows + row_of.shape[1])),
    )(row_of, weight, *blocks)


def forward_kernel(*refs):
    ins, (gate_hbm, up_hbm, down_hbm) = peer_blocks(refs[:8]), refs[8:11]
    outs, (rows_ref, hidden_ref, slope_ref, silu_ref) = refs[11:15], refs[15:19]
    gate_w, up_w, down_w, sems = refs[19:]
    loads = [
        pltpu.make_async_copy(src, dst, sems.at[i])
        for i, (src, dst) in enumerate(((gate_hbm, gate_w), (up_hbm, up_w), (down_hbm, down_w)))
    ]
    for load in loads:
        load.start()
    block = ins[0].shape[0]
    for j, r in enumerate(ins):
        rows_ref[j * block : (j + 1) * block, :] = r[...]
    loads[0].wait()
    loads[1].wait()
    for n in range(0, hidden_ref.shape[1], LANES):
        cols = slice(n, n + LANES)
        gate = dot(rows_ref[...], gate_w[:, cols])
        up = dot(rows_ref[...], up_w[:, cols])
        sigma = jax.nn.sigmoid(gate)
        silu = gate * sigma
        silu_ref[:, cols] = silu
        slope_ref[:, cols] = up * (sigma * (1.0 + gate * (1.0 - sigma)))
        hidden_ref[:, cols] = (silu * up).astype(BF16)
    loads[2].wait()
    for n in range(0, rows_ref.shape[1], LANES):
        cols = slice(n, n + LANES)
        result = dot(hidden_ref[...], down_w[:, cols]).astype(BF16)
        for out, (lo, hi) in zip(outs, GROUPS):
            out[:, cols] = result[lo * block : hi * block]


def forward(pieces, w_gate, w_up, w_down):
    block, width = pieces[4].shape
    ff = w_gate.shape[1]
    rows = len(PEERS) * block
    full = lambda shape, kind: jax.ShapeDtypeStruct(shape, kind)
    return pl.pallas_call(
        forward_kernel,
        out_shape=[full(((hi - lo) * block, width), BF16) for lo, hi in GROUPS]
        + [full((rows, width), BF16), full((rows, ff), BF16), full((rows, ff), F32), full((rows, ff), F32)],
        in_specs=[whole()] * 8 + [anywhere()] * 3,
        out_specs=[whole()] * 8,
        scratch_shapes=[
            pltpu.VMEM((width, ff), BF16),
            pltpu.VMEM((width, ff), BF16),
            pltpu.VMEM((ff, width), BF16),
            pltpu.SemaphoreType.DMA((3,)),
        ],
        compiler_params=params(),
        cost_estimate=cost(6 * rows * width * ff, 6 * width * ff + 8 * rows * width),
    )(*pieces, w_gate, w_up, w_down)


def gradient(to, k, part, rows_ref, outr_ref, back_ref, hidden_ref, store):
    cols = pl.ds(pl.multiple_of(to[k] * part, part), part)
    mine, outs = rows_ref[:, cols], outr_ref[:, cols]
    wide = back_ref.shape[1]
    for n in range(0, wide, LANES):
        store(slice(n, n + LANES), dot(mine, back_ref[:, n : n + LANES], ((0,), (0,))).astype(BF16))
    for n in range(0, hidden_ref.shape[1], LANES):
        store(
            slice(wide + n, wide + n + LANES),
            dot(outs, hidden_ref[:, n : n + LANES], ((0,), (0,))).astype(BF16),
        )


def backward_kernel(part, to, *refs):
    ins, (down_w, rows_ref, hidden_ref, slope_ref, silu_ref) = peer_blocks(refs[:8]), refs[8:13]
    far_a, far_b, outr_ref, back_ref = refs[13:]
    block = ins[0].shape[0]
    for j, r in enumerate(ins):
        outr_ref[j * block : (j + 1) * block, :] = r[...]
    ff = hidden_ref.shape[1]
    for n in range(0, ff, LANES):
        cols = slice(n, n + LANES)
        hidden_grad = dot(outr_ref[...], down_w[cols, :], ((1,), (1,)))
        back_ref[:, cols] = (hidden_grad * slope_ref[:, cols]).astype(BF16)
        back_ref[:, ff + n : ff + n + LANES] = (hidden_grad * silu_ref[:, cols]).astype(BF16)

    def store(cols, value):
        far_a[:, cols] = value[: part // 2]
        far_b[:, cols] = value[part // 2 :]

    gradient(to, 2, part, rows_ref, outr_ref, back_ref, hidden_ref, store)


def backward(to, pieces, w_down, rows, hidden, slope, silu, ndp):
    block, width = pieces[4].shape
    ff = hidden.shape[1]
    count = rows.shape[0]
    part = width // ndp
    full = lambda shape: jax.ShapeDtypeStruct(shape, BF16)
    return pl.pallas_call(
        functools.partial(backward_kernel, part),
        out_shape=[full((part // 2, 3 * ff)), full((part // 2, 3 * ff)), full((count, width)), full((count, 2 * ff))],
        in_specs=[pl.BlockSpec(memory_space=pltpu.SMEM)] + [whole()] * 8 + [whole()] * 5,
        out_specs=[whole()] * 4,
        compiler_params=params(),
        cost_estimate=cost(2 * count * width * ff + 6 * count * part * ff, 2 * width * ff + 10 * count * width),
    )(to, *pieces, w_down, rows, hidden, slope, silu)


def shares_kernel(part, to, rows_ref, outr_ref, back_ref, hidden_ref, right_a, right_b, left_a, left_b, me):
    def both(a, b):
        def store(cols, value):
            a[:, cols] = value[: part // 2]
            b[:, cols] = value[part // 2 :]

        return store

    def own(cols, value):
        me[:, cols] = value

    gradient(to, 1, part, rows_ref, outr_ref, back_ref, hidden_ref, both(right_a, right_b))
    gradient(to, 3, part, rows_ref, outr_ref, back_ref, hidden_ref, both(left_a, left_b))
    gradient(to, 0, part, rows_ref, outr_ref, back_ref, hidden_ref, own)


def shares(to, rows, outr, back, hidden, ndp):
    part = rows.shape[1] // ndp
    wide = back.shape[1] + hidden.shape[1]
    half = jax.ShapeDtypeStruct((part // 2, wide), BF16)
    return pl.pallas_call(
        functools.partial(shares_kernel, part),
        out_shape=[half] * 4 + [jax.ShapeDtypeStruct((part, wide), BF16)],
        in_specs=[pl.BlockSpec(memory_space=pltpu.SMEM)] + [whole()] * 4,
        out_specs=[whole()] * 5,
        compiler_params=params(),
        cost_estimate=cost(6 * rows.shape[0] * part * wide, 2 * rows.size * 4),
    )(to, rows, outr, back, hidden)


def terms_kernel(block, row_ref, weight_ref, *refs):
    ins, out, pick, held = peer_blocks(refs[:8]), refs[8], refs[9], refs[10]
    for j, r in enumerate(ins):
        match = match_rows(row_ref, j, block)
        span = slice(j * block, (j + 1) * block)
        pick[span, :] = jnp.where(match, 1.0, 0.0).astype(BF16)
        weight = jnp.sum(jnp.where(match, weight_ref[j : j + 1, :], 0.0), axis=1, keepdims=True)
        held[span, :] = (weight * r[...].astype(F32)).astype(BF16)
    for n in range(0, out.shape[1], LANES):
        out[:, n : n + LANES] = dot(pick[...], held[:, n : n + LANES], ((0,), (0,))).astype(BF16)


def token_terms(row_of, weight, pieces):
    block, width = pieces[4].shape
    rows = len(PEERS) * block
    count = row_of.shape[1]
    return pl.pallas_call(
        functools.partial(terms_kernel, block),
        out_shape=jax.ShapeDtypeStruct((count, width), BF16),
        in_specs=[whole()] * 2 + [whole()] * 8,
        out_specs=whole(),
        scratch_shapes=[pltpu.VMEM((rows, count), BF16), pltpu.VMEM((rows, width), BF16)],
        compiler_params=params(),
        cost_estimate=cost(2 * rows * count * width, 2 * width * (rows + count)),
    )(row_of, weight, *pieces)


def total_kernel(ff, me, left_a, left_b, right_a, right_b, gate, up, down):
    half = left_a.shape[0]
    for i, (left, right) in enumerate(((left_a, right_a), (left_b, right_b))):
        span = slice(i * half, (i + 1) * half)
        for k in range(3):
            cols = slice(k * ff, (k + 1) * ff)
            total = me[span, cols].astype(F32) + left[:, cols].astype(F32) + right[:, cols].astype(F32)
            if k == 0:
                gate[span, :] = total.astype(BF16)
            elif k == 1:
                up[span, :] = total.astype(BF16)
            else:
                down[:, span] = total.T.astype(BF16)


def totals(me, left_a, left_b, right_a, right_b):
    part, wide = me.shape
    ff = wide // 3
    return pl.pallas_call(
        functools.partial(total_kernel, ff),
        out_shape=[jax.ShapeDtypeStruct(s, BF16) for s in ((part, ff), (part, ff), (ff, part))],
        in_specs=[whole()] * 5,
        out_specs=[whole()] * 3,
        compiler_params=params(),
        cost_estimate=cost(3 * me.size, 8 * me.size),
    )(me, left_a, left_b, right_a, right_b)


def local(tokens, expert_ids, probs, trade, gate_weight, up_weight, down_weight, out_grad):
    tok_count = tokens.shape[0]
    top_count = expert_ids.shape[1]
    ny, nz, nc = (lax.axis_size(a) for a in EXPERT)
    experts = ny * nz * nc
    halfway = experts // 2
    cap = 5 * tok_count * top_count // (4 * experts)
    peers = ny * nc
    block = nz * cap
    ndp = lax.axis_size("dp")
    my, mz, mc, here = (lax.axis_index(a) for a in EXPERT + ("dp",))

    blocks = ring_gather(tokens, Z)
    raw = jnp.concatenate([expert_ids.astype(F32).T, probs.T], axis=0)
    info = jnp.stack([raw if k == 0 else turn(raw, Z, -k) for k in ring_order(nz)])
    all_grads = lax.all_gather(out_grad, Z, axis=0, tiled=True)

    steps = jnp.asarray([p[0] for p in PEERS], I32)
    other = jnp.asarray([p[1] for p in PEERS], I32)
    device = ((my + steps + ny) % ny) * (nz * nc) + mz * nc + jnp.bitwise_xor(mc, other)
    numbers = jnp.arange(halfway, dtype=I32)
    traded = jnp.any(((device % halfway)[:, None] == numbers) & (trade == 1), axis=1)
    expert = jnp.where(traded, jnp.bitwise_xor(device, halfway), device).astype(F32)
    hits = info[None, :, :top_count] == expert[:, None, None, None]
    named = jnp.any(hits, axis=2)
    weight = jnp.sum(jnp.where(hits, info[None, :, top_count:], 0.0), axis=2)
    before = (
        lax.broadcasted_iota(I32, (tok_count, tok_count), 0)
        < lax.broadcasted_iota(I32, (tok_count, tok_count), 1)
    ).astype(BF16)
    rank = dot(named.astype(BF16).reshape(peers * nz, tok_count), before).reshape(named.shape)
    near = jnp.asarray(ring_order(nz), I32)
    source = (mz + near + nz) % nz
    row_of = jnp.where(named, rank + (source * cap).astype(F32)[:, None], -1.0)
    place = ((jnp.arange(nz, dtype=I32)[:, None] == source[None, :]) * jnp.arange(nz, dtype=I32)).sum(1)
    flat = lambda a: a.reshape(peers, nz * tok_count)
    ring_rows = flat(row_of)
    z_rows, z_weight = flat(row_of[:, place]), flat(weight[:, place])

    w_gate, w_up, w_down = gate_weight[0], up_weight[0], down_weight[0]
    expert_pieces = swap(*pick_rows(ring_rows, z_weight, blocks, block, False))
    out_pieces = swap(*pick_rows(z_rows, z_weight, [all_grads], block, True))
    *expert_out, rows, hidden, slope, silu = forward(expert_pieces, w_gate, w_up, w_down)

    to = (here + jnp.arange(ndp, dtype=I32)) % ndp
    far_a, far_b, outr, back = backward(to, out_pieces, w_down, rows, hidden, slope, silu, ndp)
    from_left, from_right = turn(far_a, "dp", 1), turn(far_b, "dp", -1)
    right_a, right_b, left_a, left_b, me = shares(to, rows, outr, back, hidden, ndp)
    left_low, right_high = turn(right_b, "dp", 1), turn(left_a, "dp", -1)
    add = lambda a, b: (a.astype(F32) + b.astype(F32)).astype(BF16)
    left_high = turn(add(right_a, from_left), "dp", 1)
    right_low = turn(add(left_b, from_right), "dp", -1)
    gate_part, up_part, down_part = totals(me, left_high, left_low, right_high, right_low)

    returned = swap(*expert_out)
    combined = lax.psum_scatter(token_terms(z_rows, z_weight, returned), Z, scatter_dimension=0, tiled=True)
    return combined, gate_part[None], up_part[None], down_part[None]


def solution(mesh):
    finer = Mesh(mesh.devices.reshape(mesh.shape["dp"], 4, 8, 2), DP_EXPERT)
    rows = P(DP_EXPERT, None)
    stored = P(EXPERT, None, None)
    return jax.shard_map(
        local,
        mesh=finer,
        in_specs=(rows, rows, rows, P(), stored, stored, stored, rows),
        out_specs=(rows, P(EXPERT, "dp", None), P(EXPERT, "dp", None), P(EXPERT, None, "dp")),
        check_vma=False,
    )
```

```python
import functools

import jax
import jax.numpy as jnp
from jax import lax
from jax.experimental import pallas as pl
from jax.experimental.pallas import tpu as pltpu
from jax.sharding import Mesh
from jax.sharding import PartitionSpec as P

Y, Z, C = "expert_y", "expert_z", "expert_c"
EXPERT = (Y, Z, C)
DP_EXPERT = ("dp",) + EXPERT
F32, BF16, I32 = jnp.float32, jnp.bfloat16, jnp.int32
LANES = 256
WIDE = 512


def dot(a, b, dims=((1,), (0,))):
    return lax.dot_general(a, b, (dims, ((), ())), preferred_element_type=F32)


def turn(a, axis, step):
    n = lax.axis_size(axis)
    return lax.ppermute(a, axis, [(i, (i + step) % n) for i in range(n)])


def swap(a):
    peers = lax.axis_size((Y, C))
    return lax.all_to_all(a.reshape(peers, -1, a.shape[1]), (Y, C), 0, 0, tiled=True).reshape(a.shape)


def params():
    return pltpu.CompilerParams(vmem_limit_bytes=56 * 2**20)


def cost(flops, moved):
    return pl.CostEstimate(flops=flops, bytes_accessed=moved, transcendentals=0)


def whole():
    return pl.BlockSpec(memory_space=pltpu.VMEM)


def smem():
    return pl.BlockSpec(memory_space=pltpu.SMEM)


def anywhere():
    return pl.BlockSpec(memory_space=pl.ANY)


def fixed(a):
    return pl.BlockSpec(a.shape, lambda n: (0,) * a.ndim)


def columns(a, wide):
    return pl.BlockSpec((a.shape[0], wide), lambda n: (0, n))


def start_loads(pairs, sems):
    loads = [pltpu.make_async_copy(src, dst, sems.at[i]) for i, (src, dst) in enumerate(pairs)]
    for load in loads:
        load.start()
    return loads


def pick_kernel(pick, *refs):
    picked = dot(pick[...], refs[-2][...])
    refs[-1][...] = (refs[0][...] * picked if len(refs) == 3 else picked).astype(BF16)


def pick_rows(pick, weight, tokens):
    rows, count = pick.shape
    out = jax.ShapeDtypeStruct((rows, tokens.shape[1]), BF16)
    return pl.pallas_call(
        pick_kernel,
        grid=(tokens.shape[1] // WIDE,),
        out_shape=out,
        in_specs=[fixed(pick)] + [fixed(w) for w in weight] + [columns(tokens, WIDE)],
        out_specs=columns(out, WIDE),
        compiler_params=params(),
        cost_estimate=cost(2 * pick.size * tokens.shape[1], 2 * (pick.size + tokens.size + out.size)),
    )(pick, *weight, tokens)


def terms_kernel(pick, weight, rows, out):
    held = (weight[...] * rows[...].astype(F32)).astype(BF16)
    out[...] = dot(pick[...], held).astype(BF16)


def token_terms(pick, weight, rows):
    out = jax.ShapeDtypeStruct((pick.shape[0], rows.shape[1]), BF16)
    return pl.pallas_call(
        terms_kernel,
        grid=(rows.shape[1] // WIDE,),
        out_shape=out,
        in_specs=[fixed(pick), fixed(weight), columns(rows, WIDE)],
        out_specs=columns(out, WIDE),
        compiler_params=params(),
        cost_estimate=cost(2 * pick.size * rows.shape[1], 2 * (pick.size + rows.size + out.size)),
    )(pick, weight, rows)


def hidden_kernel(rows_hbm, gate_hbm, up_hbm, hidden_ref, slope_ref, silu_ref, rows_ref, gate_w, up_w, sems):
    loads = start_loads(((rows_hbm, rows_ref), (gate_hbm, gate_w), (up_hbm, up_w)), sems)
    loads[0].wait()
    loads[1].wait()
    for n in range(0, hidden_ref.shape[1], LANES):
        cols = slice(n, n + LANES)
        gate = dot(rows_ref[...], gate_w[:, cols])
        if n == 0:
            loads[2].wait()
        up = dot(rows_ref[...], up_w[:, cols])
        sigma = jax.nn.sigmoid(gate)
        silu = gate * sigma
        silu_ref[:, cols] = silu
        slope_ref[:, cols] = up * (sigma * (1.0 + gate * (1.0 - sigma)))
        hidden_ref[:, cols] = (silu * up).astype(BF16)


def hidden_units(rows, w_gate, w_up):
    count = rows.shape[0]
    width, ff = w_gate.shape
    args = (rows, w_gate, w_up)
    return pl.pallas_call(
        hidden_kernel,
        out_shape=[jax.ShapeDtypeStruct((count, ff), kind) for kind in (BF16, F32, F32)],
        in_specs=[anywhere()] * 3,
        out_specs=[whole()] * 3,
        scratch_shapes=[pltpu.VMEM(a.shape, BF16) for a in args] + [pltpu.SemaphoreType.DMA((3,))],
        compiler_params=params(),
        cost_estimate=cost(4 * count * width * ff, 4 * width * ff + 2 * count * (width + 5 * ff)),
    )(*args)


def outputs_kernel(rows_ref, hidden_ref, down_w, out, rows_t, hidden_t):
    for n in range(0, out.shape[1], LANES):
        cols = slice(n, n + LANES)
        out[:, cols] = dot(hidden_ref[...], down_w[:, cols]).astype(BF16)
        rows_t[cols, :] = rows_ref[:, cols].T
    hidden_t[...] = hidden_ref[...].T


def outputs(rows, hidden, w_down):
    count, ff = hidden.shape
    width = w_down.shape[1]
    return pl.pallas_call(
        outputs_kernel,
        out_shape=[jax.ShapeDtypeStruct(shape, BF16) for shape in ((count, width), (width, count), (ff, count))],
        in_specs=[whole()] * 3,
        out_specs=[whole()] * 3,
        compiler_params=params(),
        cost_estimate=cost(2 * count * width * ff, 2 * width * (ff + 3 * count)),
    )(rows, hidden, w_down)


def down_kernel(hidden_t, outs, down):
    part = down.shape[2]
    for d in range(down.shape[0]):
        down[d] = dot(hidden_t[...], outs[:, d * part : (d + 1) * part]).astype(BF16)


def down_terms(hidden_t, outs, ndp):
    ff, count = hidden_t.shape
    width = outs.shape[1]
    return pl.pallas_call(
        down_kernel,
        out_shape=jax.ShapeDtypeStruct((ndp, ff, width // ndp), BF16),
        in_specs=[whole()] * 2,
        out_specs=whole(),
        compiler_params=params(),
        cost_estimate=cost(2 * count * ff * width, 2 * (count + ff) * width),
    )(hidden_t, outs)


def store_halves(a, b, cols, value):
    half = a.shape[0]
    a[:, cols] = value[:half]
    b[:, cols] = value[half:]


def share_columns(at, part):
    return pl.ds(pl.multiple_of(at * part, part), part)


def gate_up_share(mine, back_ref, store):
    for n in range(0, back_ref.shape[1], LANES):
        cols = slice(n, n + LANES)
        store(cols, dot(mine, back_ref[:, cols]).astype(BF16))


def backward_kernel(part, to, *refs):
    hbm, (far_a, far_b, back_ref) = refs[:5], refs[5:8]
    sems, held = refs[-1], refs[8:-1]
    loads = start_loads(tuple(zip(hbm, held)), sems)
    outr_ref, down_t, slope_ref, silu_ref, rows_t = held
    ff = down_t.shape[1]
    for load in loads[:4]:
        load.wait()
    for n in range(0, ff, LANES):
        cols = slice(n, n + LANES)
        hidden_grad = dot(outr_ref[...], down_t[:, cols])
        back_ref[:, cols] = (hidden_grad * slope_ref[:, cols]).astype(BF16)
        back_ref[:, ff + n : ff + n + LANES] = (hidden_grad * silu_ref[:, cols]).astype(BF16)
    loads[4].wait()
    gate_up_share(rows_t[share_columns(to[2], part), :], back_ref, functools.partial(store_halves, far_a, far_b))


def backward(to, outr, down_t, slope, silu, rows_t, ndp):
    count, width = outr.shape
    ff = down_t.shape[1]
    part = width // ndp
    full = lambda shape: jax.ShapeDtypeStruct(shape, BF16)
    piece = full((part // 2, 2 * ff))
    args = (outr, down_t, slope, silu, rows_t)
    return pl.pallas_call(
        functools.partial(backward_kernel, part),
        out_shape=[piece, piece, full((count, 2 * ff))],
        in_specs=[smem()] + [anywhere()] * len(args),
        out_specs=[whole()] * 3,
        scratch_shapes=[pltpu.VMEM(a.shape, a.dtype) for a in args] + [pltpu.SemaphoreType.DMA((len(args),))],
        compiler_params=params(),
        cost_estimate=cost(2 * count * width * ff + 4 * count * part * ff, 2 * width * ff + 10 * count * width),
    )(to, *args)


def shares_kernel(part, to, rows_t, back_ref, right_a, right_b, left_a, left_b, me):
    def own(cols, value):
        me[:, cols] = value

    stores = [functools.partial(store_halves, right_a, right_b), functools.partial(store_halves, left_a, left_b), own]
    for k, store in zip((1, 3, 0), stores):
        gate_up_share(rows_t[share_columns(to[k], part), :], back_ref, store)


def shares(to, rows_t, back, ndp):
    count, wide = back.shape
    part = rows_t.shape[0] // ndp
    half = jax.ShapeDtypeStruct((part // 2, wide), BF16)
    return pl.pallas_call(
        functools.partial(shares_kernel, part),
        out_shape=[half] * 4 + [jax.ShapeDtypeStruct((part, wide), BF16)],
        in_specs=[smem()] + [whole()] * 2,
        out_specs=[whole()] * 5,
        compiler_params=params(),
        cost_estimate=cost(6 * count * part * wide, 2 * (rows_t.size + back.size + 3 * part * wide)),
    )(to, rows_t, back)


def over_ring(far_a, far_b, right_a, right_b, left_a, left_b, axis):
    add = lambda a, b: (a.astype(F32) + b.astype(F32)).astype(BF16)
    from_left, from_right = turn(far_a, axis, 1), turn(far_b, axis, -1)
    left_high, right_low = turn(right_b, axis, 1), turn(left_a, axis, -1)
    left_low = turn(add(right_a, from_left), axis, 1)
    right_high = turn(add(left_b, from_right), axis, -1)
    return left_low, left_high, right_low, right_high


def total_kernel(me, left_low, left_high, right_low, right_high, *outs):
    half = left_low.shape[0]
    wide = outs[0].shape[1]
    for i, (left, right) in enumerate(((left_low, right_low), (left_high, right_high))):
        span = slice(i * half, (i + 1) * half)
        for k, out in enumerate(outs):
            cols = slice(k * wide, (k + 1) * wide)
            total = me[span, cols].astype(F32) + left[:, cols].astype(F32) + right[:, cols].astype(F32)
            out[span, :] = total.astype(BF16)


def totals(me, others, count):
    rows, wide = me.shape
    return pl.pallas_call(
        total_kernel,
        out_shape=[jax.ShapeDtypeStruct((rows, wide // count), BF16)] * count,
        in_specs=[whole()] * 5,
        out_specs=[whole()] * count,
        compiler_params=params(),
        cost_estimate=cost(3 * me.size, 8 * me.size),
    )(me, *others)


def local(tokens, expert_ids, probs, trade, gate_weight, up_weight, down_weight, out_grad):
    tok_count, width = tokens.shape
    top_count = expert_ids.shape[1]
    ny, nz, nc = (lax.axis_size(a) for a in EXPERT)
    peers = ny * nc
    halfway = ny * nz * nc // 2
    cap = 5 * tok_count * top_count // (4 * ny * nz * nc)
    block = nz * cap
    rows = peers * block
    ndp = lax.axis_size("dp")
    mz, here = lax.axis_index(Z), lax.axis_index("dp")
    after = lambda arrays, *first: lax.optimization_barrier((arrays,) + first)[0]

    all_tokens = lax.all_gather(tokens, Z, axis=0, tiled=True)

    raw = jnp.concatenate([expert_ids.astype(F32).T, probs.T], axis=0)
    near = jnp.stack([raw] + [turn(raw, Z, -k) for k in range(1, nz)])
    info = jnp.roll(near, mz, axis=0)

    p = jnp.arange(peers, dtype=I32)
    device = p // nc * (nz * nc) + mz * nc + p % nc
    numbers = jnp.arange(halfway, dtype=I32)
    traded = jnp.any(((device % halfway)[:, None] == numbers) & (trade == 1), axis=1)
    expert = jnp.where(traded, jnp.bitwise_xor(device, halfway), device).astype(F32)
    hits = info[None, :, :top_count] == expert[:, None, None, None]
    named = jnp.any(hits, axis=2)
    weight = jnp.sum(jnp.where(hits, info[None, :, top_count:], 0.0), axis=2)
    before = (
        lax.broadcasted_iota(I32, (tok_count, tok_count), 0)
        < lax.broadcasted_iota(I32, (tok_count, tok_count), 1)
    ).astype(BF16)
    rank = dot(named.astype(BF16).reshape(peers * nz, tok_count), before).reshape(named.shape)
    row_of = jnp.where(named, rank + (jnp.arange(nz, dtype=F32) * cap)[:, None], -1.0)
    flat = lambda a: a.reshape(peers, 1, nz * tok_count)
    match = flat(row_of) == jnp.arange(block, dtype=F32)[None, :, None]
    pick = match.astype(BF16).reshape(rows, nz * tok_count)
    row_weight = jnp.sum(jnp.where(match, flat(weight), 0.0), axis=2).reshape(rows, 1)
    spread = pick.T
    w_down = down_weight[0]
    down_t = w_down.T
    all_grads = lax.all_gather(after(out_grad, pick, row_weight, spread, down_t), Z, axis=0, tiled=True)

    w_gate, w_up = gate_weight[0], up_weight[0]
    expert_rows = swap(pick_rows(pick, [], all_tokens))
    hidden, slope, silu = hidden_units(expert_rows, w_gate, w_up)
    picked = pick_rows(pick, [row_weight], after(all_grads, hidden))
    out_rows = swap(picked)
    expert_out, rows_t, hidden_t = outputs(expert_rows, after(hidden, picked), w_down)
    returned = swap(expert_out)

    to = (here + jnp.arange(ndp, dtype=I32)) % ndp
    down = down_terms(hidden_t, out_rows, ndp)
    down_part = lax.psum_scatter(down, "dp", scatter_dimension=0, tiled=True)
    *far, back = backward(to, after(out_rows, down), down_t, slope, silu, rows_t, ndp)
    *near, me = shares(to, rows_t, back, ndp)
    gate_part, up_part = totals(me, over_ring(*far, *near, "dp"), 2)

    returned = after(returned, near)
    combined = lax.psum_scatter(token_terms(spread, row_weight, returned), Z, scatter_dimension=0, tiled=True)
    return combined, gate_part[None], up_part[None], down_part


def solution(mesh):
    finer = Mesh(mesh.devices.reshape(mesh.shape["dp"], 4, 8, 2), DP_EXPERT)
    rows = P(DP_EXPERT, None)
    stored = P(EXPERT, None, None)
    return jax.shard_map(
        local,
        mesh=finer,
        in_specs=(rows, rows, rows, P(), stored, stored, stored, rows),
        out_specs=(rows, P(EXPERT, "dp", None), P(EXPERT, "dp", None), P(EXPERT, None, "dp")),
        check_vma=False,
    )
```

```python
import functools

import jax
import jax.numpy as jnp
from jax import lax
from jax.experimental import pallas as pl
from jax.experimental.pallas import tpu as pltpu
from jax.sharding import Mesh
from jax.sharding import PartitionSpec as P

Y, Z, C = "expert_y", "expert_z", "expert_c"
EXPERT = (Y, Z, C)
DP_EXPERT = ("dp",) + EXPERT
F32, BF16, I32 = jnp.float32, jnp.bfloat16, jnp.int32
LANES = 256
WIDE = 512


def dot(a, b, dims=((1,), (0,))):
    return lax.dot_general(a, b, (dims, ((), ())), preferred_element_type=F32)


def turn(a, axis, step):
    n = lax.axis_size(axis)
    return lax.ppermute(a, axis, [(i, (i + step) % n) for i in range(n)])


def swap(a):
    peers = lax.axis_size((Y, C))
    return lax.all_to_all(a.reshape(peers, -1, a.shape[1]), (Y, C), 0, 0, tiled=True).reshape(a.shape)


def params():
    return pltpu.CompilerParams(vmem_limit_bytes=56 * 2**20)


def cost(flops, moved):
    return pl.CostEstimate(flops=flops, bytes_accessed=moved, transcendentals=0)


def whole():
    return pl.BlockSpec(memory_space=pltpu.VMEM)


def smem():
    return pl.BlockSpec(memory_space=pltpu.SMEM)


def anywhere():
    return pl.BlockSpec(memory_space=pl.ANY)


def fixed(a):
    return pl.BlockSpec(a.shape, lambda n: (0,) * a.ndim)


def columns(a, wide):
    return pl.BlockSpec((a.shape[0], wide), lambda n: (0, n))


def start_loads(pairs, sems):
    loads = [pltpu.make_async_copy(src, dst, sems.at[i]) for i, (src, dst) in enumerate(pairs)]
    for load in loads:
        load.start()
    return loads


def pick_kernel(pick, *refs):
    picked = dot(pick[...], refs[-2][...])
    refs[-1][...] = (refs[0][...] * picked if len(refs) == 3 else picked).astype(BF16)


def pick_rows(pick, weight, tokens):
    rows, count = pick.shape
    out = jax.ShapeDtypeStruct((rows, tokens.shape[1]), BF16)
    return pl.pallas_call(
        pick_kernel,
        grid=(tokens.shape[1] // WIDE,),
        out_shape=out,
        in_specs=[fixed(pick)] + [fixed(w) for w in weight] + [columns(tokens, WIDE)],
        out_specs=columns(out, WIDE),
        compiler_params=params(),
        cost_estimate=cost(2 * pick.size * tokens.shape[1], 2 * (pick.size + tokens.size + out.size)),
    )(pick, *weight, tokens)


def column_loads(src, dst, sems, wide):
    spans = [slice(n, n + wide) for n in range(0, src.shape[1], wide)]
    return spans, start_loads([(src.at[:, c], dst.at[:, c]) for c in spans], sems)


def terms_kernel(pick, weight, rows_hbm, out, rows_ref, sems):
    spans, loads = column_loads(rows_hbm, rows_ref, sems, WIDE)
    for cols, load in zip(spans, loads):
        load.wait()
        held = (weight[...] * rows_ref[:, cols].astype(F32)).astype(BF16)
        out[:, cols] = dot(pick[...], held).astype(BF16)


def token_terms(pick, weight, rows):
    out = jax.ShapeDtypeStruct((pick.shape[0], rows.shape[1]), BF16)
    return pl.pallas_call(
        terms_kernel,
        out_shape=out,
        in_specs=[whole(), whole(), pl.BlockSpec(memory_space=pltpu.HBM)],
        out_specs=whole(),
        scratch_shapes=[pltpu.VMEM(rows.shape, BF16), pltpu.SemaphoreType.DMA((rows.shape[1] // WIDE,))],
        compiler_params=params(),
        cost_estimate=cost(2 * pick.size * rows.shape[1], 2 * (pick.size + rows.size + out.size)),
    )(pick, weight, rows)


def hidden_kernel(rows_hbm, gate_hbm, up_hbm, hidden_ref, slope_ref, silu_ref, rows_ref, gate_w, up_w, sems):
    loads = start_loads(((rows_hbm, rows_ref), (gate_hbm, gate_w), (up_hbm, up_w)), sems)
    loads[0].wait()
    loads[1].wait()
    for n in range(0, hidden_ref.shape[1], LANES):
        cols = slice(n, n + LANES)
        gate = dot(rows_ref[...], gate_w[:, cols])
        if n == 0:
            loads[2].wait()
        up = dot(rows_ref[...], up_w[:, cols])
        sigma = jax.nn.sigmoid(gate)
        silu = gate * sigma
        silu_ref[:, cols] = silu
        slope_ref[:, cols] = up * (sigma * (1.0 + gate * (1.0 - sigma)))
        hidden_ref[:, cols] = (silu * up).astype(BF16)


def hidden_units(rows, w_gate, w_up):
    count = rows.shape[0]
    width, ff = w_gate.shape
    args = (rows, w_gate, w_up)
    return pl.pallas_call(
        hidden_kernel,
        out_shape=[jax.ShapeDtypeStruct((count, ff), kind) for kind in (BF16, F32, F32)],
        in_specs=[anywhere()] * 3,
        out_specs=[whole()] * 3,
        scratch_shapes=[pltpu.VMEM(a.shape, BF16) for a in args] + [pltpu.SemaphoreType.DMA((3,))],
        compiler_params=params(),
        cost_estimate=cost(4 * count * width * ff, 4 * width * ff + 2 * count * (width + 5 * ff)),
    )(*args)


def outputs_kernel(rows_ref, hidden_ref, down_w, out, rows_t, hidden_t):
    for n in range(0, out.shape[1], LANES):
        cols = slice(n, n + LANES)
        out[:, cols] = dot(hidden_ref[...], down_w[:, cols]).astype(BF16)
        rows_t[cols, :] = rows_ref[:, cols].T
    hidden_t[...] = hidden_ref[...].T


def outputs(rows, hidden, w_down):
    count, ff = hidden.shape
    width = w_down.shape[1]
    return pl.pallas_call(
        outputs_kernel,
        out_shape=[jax.ShapeDtypeStruct(shape, BF16) for shape in ((count, width), (width, count), (ff, count))],
        in_specs=[whole()] * 3,
        out_specs=[whole()] * 3,
        compiler_params=params(),
        cost_estimate=cost(2 * count * width * ff, 2 * width * (ff + 3 * count)),
    )(rows, hidden, w_down)


def down_kernel(hidden_t, outs_hbm, down, outs, sems):
    spans, loads = column_loads(outs_hbm, outs, sems, down.shape[2])
    for d, (cols, load) in enumerate(zip(spans, loads)):
        load.wait()
        down[d] = dot(hidden_t[...], outs[:, cols]).astype(BF16)


def down_terms(hidden_t, outs, ndp):
    ff, count = hidden_t.shape
    width = outs.shape[1]
    return pl.pallas_call(
        down_kernel,
        out_shape=jax.ShapeDtypeStruct((ndp, ff, width // ndp), BF16),
        in_specs=[whole(), pl.BlockSpec(memory_space=pltpu.HBM)],
        out_specs=whole(),
        scratch_shapes=[pltpu.VMEM(outs.shape, BF16), pltpu.SemaphoreType.DMA((ndp,))],
        compiler_params=params(),
        cost_estimate=cost(2 * count * ff * width, 2 * (count + ff) * width),
    )(hidden_t, outs)


def store_halves(a, b, cols, value):
    half = a.shape[0]
    a[:, cols] = value[:half]
    b[:, cols] = value[half:]


def share_columns(at, part):
    return pl.ds(pl.multiple_of(at * part, part), part)


def gate_up_share(mine, back_ref, store):
    for n in range(0, back_ref.shape[1], LANES):
        cols = slice(n, n + LANES)
        store(cols, dot(mine, back_ref[:, cols]).astype(BF16))


def backward_kernel(part, to, *refs):
    hbm, (far_a, far_b, back_ref) = refs[:5], refs[5:8]
    sems, held = refs[-1], refs[8:-1]
    loads = start_loads(tuple(zip(hbm, held)), sems)
    outr_ref, down_t, slope_ref, silu_ref, rows_t = held
    ff = down_t.shape[1]
    for load in loads[:4]:
        load.wait()
    for n in range(0, ff, LANES):
        cols = slice(n, n + LANES)
        hidden_grad = dot(outr_ref[...], down_t[:, cols])
        back_ref[:, cols] = (hidden_grad * slope_ref[:, cols]).astype(BF16)
        back_ref[:, ff + n : ff + n + LANES] = (hidden_grad * silu_ref[:, cols]).astype(BF16)
    loads[4].wait()
    gate_up_share(rows_t[share_columns(to[2], part), :], back_ref, functools.partial(store_halves, far_a, far_b))


def backward(to, outr, down_t, slope, silu, rows_t, ndp):
    count, width = outr.shape
    ff = down_t.shape[1]
    part = width // ndp
    full = lambda shape: jax.ShapeDtypeStruct(shape, BF16)
    piece = full((part // 2, 2 * ff))
    args = (outr, down_t, slope, silu, rows_t)
    return pl.pallas_call(
        functools.partial(backward_kernel, part),
        out_shape=[piece, piece, full((count, 2 * ff))],
        in_specs=[smem()] + [anywhere()] * len(args),
        out_specs=[whole()] * 3,
        scratch_shapes=[pltpu.VMEM(a.shape, a.dtype) for a in args] + [pltpu.SemaphoreType.DMA((len(args),))],
        compiler_params=params(),
        cost_estimate=cost(2 * count * width * ff + 4 * count * part * ff, 2 * width * ff + 10 * count * width),
    )(to, *args)


def shares_kernel(part, to, rows_t, back_ref, right_a, right_b, left_a, left_b, me):
    def own(cols, value):
        me[:, cols] = value

    stores = [functools.partial(store_halves, right_a, right_b), functools.partial(store_halves, left_a, left_b), own]
    for k, store in zip((1, 3, 0), stores):
        gate_up_share(rows_t[share_columns(to[k], part), :], back_ref, store)


def shares(to, rows_t, back, ndp):
    count, wide = back.shape
    part = rows_t.shape[0] // ndp
    half = jax.ShapeDtypeStruct((part // 2, wide), BF16)
    return pl.pallas_call(
        functools.partial(shares_kernel, part),
        out_shape=[half] * 4 + [jax.ShapeDtypeStruct((part, wide), BF16)],
        in_specs=[smem()] + [whole()] * 2,
        out_specs=[whole()] * 5,
        compiler_params=params(),
        cost_estimate=cost(6 * count * part * wide, 2 * (rows_t.size + back.size + 3 * part * wide)),
    )(to, rows_t, back)


def over_ring(far_a, far_b, right_a, right_b, left_a, left_b, axis):
    add = lambda a, b: (a.astype(F32) + b.astype(F32)).astype(BF16)
    from_left, from_right = turn(far_a, axis, 1), turn(far_b, axis, -1)
    left_high, right_low = turn(right_b, axis, 1), turn(left_a, axis, -1)
    left_low = turn(add(right_a, from_left), axis, 1)
    right_high = turn(add(left_b, from_right), axis, -1)
    return left_low, left_high, right_low, right_high


def total_kernel(me, left_low, left_high, right_low, right_high, *outs):
    half = left_low.shape[0]
    wide = outs[0].shape[1]
    for i, (left, right) in enumerate(((left_low, right_low), (left_high, right_high))):
        span = slice(i * half, (i + 1) * half)
        for k, out in enumerate(outs):
            cols = slice(k * wide, (k + 1) * wide)
            total = me[span, cols].astype(F32) + left[:, cols].astype(F32) + right[:, cols].astype(F32)
            out[span, :] = total.astype(BF16)


def totals(me, others, count):
    rows, wide = me.shape
    return pl.pallas_call(
        total_kernel,
        out_shape=[jax.ShapeDtypeStruct((rows, wide // count), BF16)] * count,
        in_specs=[whole()] * 5,
        out_specs=[whole()] * count,
        compiler_params=params(),
        cost_estimate=cost(3 * me.size, 8 * me.size),
    )(me, *others)


def local(tokens, expert_ids, probs, trade, gate_weight, up_weight, down_weight, out_grad):
    tok_count, width = tokens.shape
    top_count = expert_ids.shape[1]
    ny, nz, nc = (lax.axis_size(a) for a in EXPERT)
    peers = ny * nc
    halfway = ny * nz * nc // 2
    cap = 5 * tok_count * top_count // (4 * ny * nz * nc)
    block = nz * cap
    rows = peers * block
    ndp = lax.axis_size("dp")
    mz, here = lax.axis_index(Z), lax.axis_index("dp")
    after = lambda arrays, *first: lax.optimization_barrier((arrays,) + first)[0]

    all_tokens = lax.all_gather(tokens, Z, axis=0, tiled=True)

    raw = jnp.concatenate([expert_ids.astype(F32).T, probs.T], axis=0)
    near = jnp.stack([raw] + [turn(raw, Z, -k) for k in range(1, nz)])
    info = jnp.roll(near, mz, axis=0)

    p = jnp.arange(peers, dtype=I32)
    device = p // nc * (nz * nc) + mz * nc + p % nc
    numbers = jnp.arange(halfway, dtype=I32)
    traded = jnp.any(((device % halfway)[:, None] == numbers) & (trade == 1), axis=1)
    expert = jnp.where(traded, jnp.bitwise_xor(device, halfway), device).astype(F32)
    hits = info[None, :, :top_count] == expert[:, None, None, None]
    named = jnp.any(hits, axis=2)
    weight = jnp.sum(jnp.where(hits, info[None, :, top_count:], 0.0), axis=2)
    before = (
        lax.broadcasted_iota(I32, (tok_count, tok_count), 0)
        < lax.broadcasted_iota(I32, (tok_count, tok_count), 1)
    ).astype(BF16)
    rank = dot(named.astype(BF16).reshape(peers * nz, tok_count), before).reshape(named.shape)
    row_of = jnp.where(named, rank + (jnp.arange(nz, dtype=F32) * cap)[:, None], -1.0)
    flat = lambda a: a.reshape(peers, 1, nz * tok_count)
    match = flat(row_of) == jnp.arange(block, dtype=F32)[None, :, None]
    pick = match.astype(BF16).reshape(rows, nz * tok_count)
    row_weight = jnp.sum(jnp.where(match, flat(weight), 0.0), axis=2).reshape(rows, 1)
    spread = pick.T
    w_down = down_weight[0]
    down_t = w_down.T
    all_grads = lax.all_gather(after(out_grad, pick, row_weight, spread, down_t), Z, axis=0, tiled=True)

    w_gate, w_up = gate_weight[0], up_weight[0]
    expert_rows = swap(pick_rows(pick, [], all_tokens))
    hidden, slope, silu = hidden_units(expert_rows, w_gate, w_up)
    picked = pick_rows(pick, [row_weight], after(all_grads, hidden))
    out_rows = swap(picked)
    expert_out, rows_t, hidden_t = outputs(expert_rows, after(hidden, picked), w_down)
    returned = swap(expert_out)

    to = (here + jnp.arange(ndp, dtype=I32)) % ndp
    down = down_terms(hidden_t, out_rows, ndp)
    down_part = lax.psum_scatter(down, "dp", scatter_dimension=0, tiled=True)
    *far, back = backward(to, after(out_rows, down), down_t, slope, silu, rows_t, ndp)
    *near, me = shares(to, rows_t, back, ndp)
    gate_part, up_part = totals(me, over_ring(*far, *near, "dp"), 2)

    returned = after(returned, near)
    combined = lax.psum_scatter(token_terms(spread, row_weight, returned), Z, scatter_dimension=0, tiled=True)
    return combined, gate_part[None], up_part[None], down_part


def solution(mesh):
    finer = Mesh(mesh.devices.reshape(mesh.shape["dp"], 4, 8, 2), DP_EXPERT)
    rows = P(DP_EXPERT, None)
    stored = P(EXPERT, None, None)
    return jax.shard_map(
        local,
        mesh=finer,
        in_specs=(rows, rows, rows, P(), stored, stored, stored, rows),
        out_specs=(rows, P(EXPERT, "dp", None), P(EXPERT, "dp", None), P(EXPERT, None, "dp")),
        check_vma=False,
    )
```
